32 devices in a mesh: dp: 2 (over y), group: 4 (over z), expert: 4 (over x, core).
Axes of the slice: x: 2, y: 2, z: 4, core: 2. Of those that a mesh axis runs over, the one named last changes fastest.
Arguments:
- saved_inputs: bfloat16 [4096, 2688], P(('dp', 'group', 'expert')), parts along dimension 0, may hold values from -6 to 6
- out_grad: bfloat16 [4096, 2688], P(('dp', 'group', 'expert')), parts along dimension 0, may hold values from -6 to 6
- expert_ids: int32 [4096, 6], P(('dp', 'group', 'expert')), parts along dimension 0, may hold values from 0 to 15, all different within a row; in each aligned block of 128 rows (0 to 127, 128 to 255, ...) at most 56 rows name the same one
- gate_fixed: int32 [4096, 6], P(('dp', 'group', 'expert')), parts along dimension 0, may hold values from 1 to 65535
- up_values: bfloat16 [16, 2688, 928], P(('group', 'expert')), may hold values from -0.125 to 0.125
- up_scales: float32 [16, 84, 29], P(('group', 'expert')), may hold values from 0.5 to 2
- down_values: bfloat16 [16, 928, 2688], P(('group', 'expert')), may hold values from -0.125 to 0.125
- down_scales: float32 [16, 29, 84], P(('group', 'expert')), may hold values from 0.5 to 2
Outputs:
- input_grad: bfloat16 [4096, 2688], P(('dp', 'group', 'expert')), parts along dimension 0
The draws below stay inside these ranges and needn't reach their ends.
There are 2 independent parts, one for each index of `dp`. The reference program is written for one: setup_inputs(seed, part) draws one part's arguments, and reference() takes and returns one part's arrays. A program takes and returns all parts, laid end to end along the dimension named above; an argument that names none is the same for every part. Nothing has to cross between parts.
Inputs may be any that keep to these rules, and one draw needn't show every extreme that they name: `expert_ids`: each token names 6 different experts. Among the 128 tokens of one device (aligned blocks of rows), no expert is named more than 56 times, a bound that some block reaches.
All inputs are finite; a program needn't handle non-finite values.
Results may differ from the reference program's by a relative error of at most 0.0081.
Values may be sent and summed in bfloat16 or wider, within the bound.
No kernel may reach another device: no remote copies, remote signals or barrier semaphores. Data moves between devices by JAX's collectives and lax.ppermute only.
A program may use at most 128 MiB of HBM per device.

```python
import math
import jax
import jax.numpy as jnp
import numpy as np
from jax import lax

D = 2688
TOP = 6
FWIN = 928
SB = 32
TOK_DEV = 128
EXPERTS = 16
TOKENS = 2048
CAP = 56
N_GROUP = 4
N_EXPERT = 4


def with_ends(values, stream_key, smallest, largest):
    dims = values.shape
    place = [jax.random.randint(jax.random.fold_in(stream_key, axis), (), 0, dims[axis]) for axis in range(len(dims))]
    values = values.at[tuple(place)].set(smallest)
    longest = dims.index(max(dims))
    place[longest] = (place[longest] + 1) % dims[longest]
    return values.at[tuple(place)].set(largest)


def shard_levels(rng, shape, pieces, low, top_value):
    loudness, own = 1.0, jax.random.fold_in(rng, 6)
    for position, parts in pieces:
        draws = jnp.exp(jax.random.uniform(jax.random.fold_in(own, position), (parts,), jnp.float32, low / len(pieces), top_value / len(pieces)))
        loudness = loudness * jnp.repeat(draws, shape[position] // parts).reshape([-1 if axis == position else 1 for axis in range(len(shape))])
    return loudness


def shared_out(rng, own, number, rows, amount, top, reach, lean):
    sequence = jax.random.permutation(rng, amount)
    crowded, usual = load_shares(amount, rows * top, reach, lean, True), load_shares(amount, rows * top, reach, lean, False)
    places = jnp.arange(amount)

    def named(lengths, turn):
        used = int((lengths > 0).sum())
        fixed = max(1, used // 4)
        passed = fixed + (places - fixed + turn * (used - fixed)) % max(1, amount - fixed)
        return jnp.zeros((amount,), jnp.int32).at[sequence[jnp.where(places < fixed, places, passed)]].set(jnp.asarray(lengths, jnp.int32))

    lengths = jnp.where(number % 4 == 0, named(crowded, number // 4), named(usual, number - number // 4 - 1))
    mixed = jax.random.permutation(jax.random.fold_in(own, 3), amount)
    source_of, taker = mixed[0:amount // 2 * 2:2], mixed[1:amount // 2 * 2:2]
    slack = jnp.minimum(lengths[source_of] - 1, reach - lengths[taker]) // 2
    slack = jnp.where((source_of == sequence[0]) | (taker == sequence[0]) | (lengths[taker] == 0), 0, jnp.maximum(slack, 0))
    passed = jax.random.randint(jax.random.fold_in(own, 4), (amount // 2,), 0, 1 << 20) % (slack + 1)
    lengths = lengths.at[source_of].add(-passed).at[taker].add(passed)
    labels = jnp.searchsorted(jnp.cumsum(lengths), jnp.arange(rows * top), side="right").astype(jnp.int32)
    table = labels.reshape(top, rows).T
    table = table[jax.random.permutation(jax.random.fold_in(own, 1), rows)]
    turn = jax.random.randint(jax.random.fold_in(own, 2), (rows, 1), 0, top)
    return jnp.take_along_axis(table, (jnp.arange(top)[None, :] + turn) % top, axis=1)


def load_shares(amount, total, reach, skew, full):
    loads = [(1 << 20) // math.isqrt(standing ** skew) + 1 for standing in range(1, amount + 1)]
    largest = reach if full else min(reach, max(-(-total // amount), total * loads[0] // sum(loads)))
    least = 1 if total - largest >= amount - 1 else 0
    holding, rest = [largest] + [least] * (amount - 1), total - largest - least * (amount - 1)
    while rest > 0:
        free = [i for i in range(1, amount) if holding[i] < largest] or [i for i in range(1, amount) if holding[i] < reach]
        mass, remaining = sum([loads[i] for i in free]), rest
        for i in free:
            more = min(reach - holding[i], max(1, remaining * loads[i] // mass), rest)
            holding[i] = holding[i] + more
            rest = rest - more
    return np.array(holding)


def normal_values(own_key, shape, scale, reach, split=(), kind=jnp.bfloat16):
    array = scale * jax.random.normal(own_key, shape, jnp.float32)
    if split:
        array = array * shard_levels(own_key, shape, split, -0.22, 0.18)
    return jnp.clip(array, -reach, reach).astype(kind)


def setup_inputs(seed: int = 0, part: int = 0) -> dict:
    keys = jax.random.split(jax.random.key(seed), 9)
    part_splits = jax.random.split(jax.random.fold_in(keys[8], part), 9)
    saved_inputs = normal_values(part_splits[0], (TOKENS, D), 1.0, 6.0, ((0, 16),))
    out_grad = normal_values(part_splits[1], (TOKENS, D), 1.0, 6.0, ((0, 16),))
    expert_ids_keys = jax.random.split(jax.random.fold_in(part_splits[2], 1), TOKENS // TOK_DEV)
    expert_ids_turns = jax.random.permutation(jax.random.fold_in(part_splits[2], 3), TOKENS // TOK_DEV)
    expert_ids = jax.vmap(lambda own, number: shared_out(jax.random.fold_in(part_splits[2], 2), own, number, TOK_DEV, EXPERTS, TOP, CAP, 1))(expert_ids_keys, expert_ids_turns).reshape((TOKENS, TOP))
    gate_fixed = with_ends(jax.random.randint(part_splits[3], (TOKENS, TOP), 1, 65536), jax.random.fold_in(part_splits[3], 1), 1, 65535).astype(jnp.int32)
    up_values = normal_values(keys[4], (EXPERTS, D, FWIN), D ** -0.5, 0.125, ((0, 16),))
    up_scales = jnp.clip(jnp.exp(math.log(2.0) - 1.3862944 * jax.random.uniform(keys[5], (EXPERTS, D // SB, FWIN // SB), jnp.float32) ** shard_levels(keys[5], (EXPERTS, D // SB, FWIN // SB), ((0, 16),), -0.2, 0.2)), 0.5, 2.0)
    down_values = normal_values(keys[6], (EXPERTS, FWIN, D), D ** -0.5, 0.125, ((0, 16),))
    down_scales = jnp.clip(jnp.exp(math.log(2.0) - 1.3862944 * jax.random.uniform(keys[7], (EXPERTS, FWIN // SB, D // SB), jnp.float32) ** shard_levels(keys[7], (EXPERTS, FWIN // SB, D // SB), ((0, 16),), -0.2, 0.2)), 0.5, 2.0)
    return {"saved_inputs": saved_inputs, "out_grad": out_grad, "expert_ids": expert_ids, "gate_fixed": gate_fixed, "up_values": up_values, "up_scales": up_scales, "down_values": down_values, "down_scales": down_scales}


def dequant(values, scales):
    row_count, col_count = values.shape
    col_scales = jnp.repeat(scales, SB, axis=1)
    widened = values.astype(jnp.float32).reshape(row_count // SB, SB, col_count) * col_scales[:, None, :]
    return widened.reshape(row_count, col_count).astype(jnp.bfloat16)


def expert_rows(inputs, scaled, w_up, w_down):
    pre_act = jnp.dot(inputs, w_up, preferred_element_type=jnp.float32)
    hidden_grad = lax.dot_general(scaled, w_down, (((1,), (1,)), ((), ())), preferred_element_type=jnp.float32)
    pre_grad = (hidden_grad * 2.0 * jnp.maximum(pre_act, 0.0)).astype(jnp.bfloat16)
    return lax.dot_general(pre_grad, w_up, (((1,), (1,)), ((), ())), preferred_element_type=jnp.float32).astype(jnp.bfloat16)


def reference(saved_inputs, out_grad, expert_ids, gate_fixed, up_values, up_scales, down_values, down_scales):
    device_count = N_GROUP * N_EXPERT
    pair_count = TOKENS * TOP
    block_ids = expert_ids.reshape(device_count, TOK_DEV * TOP).astype(jnp.int32)
    onehot = (block_ids[:, :, None] == jnp.arange(EXPERTS, dtype=jnp.int32)[None, None, :]).astype(jnp.int32)
    earlier = jnp.cumsum(onehot, axis=1) - onehot
    slot_index = jnp.sum(earlier * onehot, axis=2).astype(jnp.int32)
    source = jnp.broadcast_to(jnp.arange(device_count, dtype=jnp.int32)[:, None], block_ids.shape)
    slot_key = ((block_ids * device_count + source) * CAP + slot_index).reshape(-1)
    table_flat = jnp.full((EXPERTS * device_count * CAP,), pair_count, dtype=jnp.int32)
    table_flat = table_flat.at[slot_key].set(jnp.arange(pair_count, dtype=jnp.int32))
    table_rows = table_flat.reshape(EXPERTS, device_count * CAP)
    gate_flat = gate_fixed.reshape(-1).astype(jnp.float32) / 65536.0

    def one_expert(total, items):
        entries, up_val, up_scl, down_val, down_scl = items
        valid = entries < pair_count
        safe = jnp.where(valid, entries, 0).astype(jnp.int32)
        token = (safe // TOP).astype(jnp.int32)
        inputs = saved_inputs[token]
        scaled = (gate_flat[safe][:, None] * out_grad[token].astype(jnp.float32)).astype(jnp.bfloat16)
        contrib = expert_rows(inputs, scaled, dequant(up_val, up_scl), dequant(down_val, down_scl))
        target = jnp.where(valid, token, TOKENS).astype(jnp.int32)
        total = total.at[target].add(contrib.astype(jnp.float32), mode="drop")
        return total, None

    start = jnp.zeros((TOKENS, D), dtype=jnp.float32)
    total, unused = lax.scan(one_expert, start, (table_rows, up_values, up_scales, down_values, down_scales))
    return total.astype(jnp.bfloat16)
```

```python
import jax
import jax.numpy as jnp
from jax import lax
from jax.sharding import Mesh, PartitionSpec as P

SB = 32
CORES = 2
AHEAD = 3


def dequant(values, scales):
    row_count, col_count = values.shape
    col_scales = jnp.repeat(scales, SB, axis=1)
    widened = (
        values.astype(jnp.float32).reshape(row_count // SB, SB, col_count) * col_scales[:, None, :]
    )
    return widened.reshape(row_count, col_count).astype(jnp.bfloat16)


def shift(value, axis, by):
    size = lax.axis_size(axis)
    return lax.ppermute(value, axis, [(i, (i + by) % size) for i in range(size)])


def expert_rows(inputs, grads, gate, w_up, w_down):
    scaled = (gate[:, None] * grads.astype(jnp.float32)).astype(jnp.bfloat16)
    pre_act = jnp.dot(inputs, w_up, preferred_element_type=jnp.float32)
    hidden_grad = lax.dot_general(
        scaled, w_down, (((1,), (1,)), ((), ())), preferred_element_type=jnp.float32
    )
    pre_grad = (hidden_grad * 2.0 * jnp.maximum(pre_act, 0.0)).astype(jnp.bfloat16)
    return lax.dot_general(
        pre_grad, w_up, (((1,), (1,)), ((), ())), preferred_element_type=jnp.float32
    ).astype(jnp.bfloat16)


def gate_columns(expert_ids, gate_fixed):
    groups, sides = lax.axis_size("group"), lax.axis_size("x")
    experts = groups * sides * CORES
    hit = expert_ids[None, :, :] == jnp.arange(experts, dtype=jnp.int32)[:, None, None]
    table = jnp.sum(jnp.where(hit, gate_fixed[None], 0), axis=2).astype(jnp.float32) / 65536.0
    table = lax.all_to_all(table, ("group", "x", "core"), split_axis=0, concat_axis=0, tiled=True)
    table = table.reshape(groups, sides, CORES, -1)
    for dim, axis in enumerate(("group", "x", "core")):
        size = lax.axis_size(axis)
        order = (lax.axis_index(axis) - jnp.arange(size)) % size
        table = jnp.take(table, order, axis=dim)
    return table


def shards(
    saved_inputs, out_grad, expert_ids, gate_fixed, up_values, up_scales, down_values, down_scales
):
    groups, sides = lax.axis_size("group"), lax.axis_size("x")
    tok_dev, width = saved_inputs.shape

    def spread(value):
        out = []
        for side in range(sides):
            there = value if side == 0 else shift(value, "x", side)
            out += [there, shift(there, "core", 1)]
        return out

    gates = gate_columns(expert_ids, gate_fixed)
    w_up = dequant(up_values[0], up_scales[0])
    w_down = dequant(down_values[0], down_scales[0])

    held = (saved_inputs, out_grad)
    reduced = []
    for step in range(groups):
        if step > AHEAD:
            held, reduced[step - AHEAD] = lax.optimization_barrier((held, reduced[step - AHEAD]))
        if step > 0:
            held = tuple(shift(value, "group", 1) for value in held)
        inputs, grads = (jnp.concatenate(spread(value), axis=0) for value in held)
        rows = expert_rows(inputs, grads, gates[step].reshape(-1), w_up, w_down)
        rows = rows.reshape(sides, CORES, tok_dev, width)
        here = rows[:, 0].astype(jnp.float32) + shift(rows[:, 1], "core", 1).astype(jnp.float32)
        part = here[0]
        for side in range(1, sides):
            part = part + shift(here[side].astype(jnp.bfloat16), "x", -side).astype(jnp.float32)
        reduced.append(part)
    total = reduced[1]
    for step in range(2, groups + 1):
        total = shift(total.astype(jnp.bfloat16), "group", 1).astype(jnp.float32)
        total = total + reduced[step % groups]
    return total.astype(jnp.bfloat16)


def solution(mesh):
    dp, groups, experts = mesh.devices.shape
    fine = Mesh(
        mesh.devices.reshape(dp, groups, experts // CORES, CORES), ("dp", "group", "x", "core")
    )
    tokens = P(("dp", "group", "x", "core"), None)
    weights = P(("group", "x", "core"), None, None)
    return jax.shard_map(
        shards,
        mesh=fine,
        in_specs=(tokens,) * 4 + (weights,) * 4,
        out_specs=tokens,
        check_vma=False,
    )
```

```python
import functools

import jax
import jax.numpy as jnp
from jax import lax
from jax.experimental import pallas as pl
from jax.experimental.pallas import tpu as pltpu
from jax.sharding import Mesh, PartitionSpec as P

SB = 32
CORES = 2
LANES = 128
BLOCKS = 2
VMEM_BYTES = 40 * 2**20
NT = (((1,), (1,)), ((), ()))


def shift(value, axis, by):
    size = lax.axis_size(axis)
    return lax.ppermute(value, axis, [(i, (i + by) % size) for i in range(size)])


def nothing(*refs):
    pass


def in_order(values):
    return pl.pallas_call(
        nothing,
        out_shape=[jax.ShapeDtypeStruct(value.shape, value.dtype) for value in values],
        in_specs=[pl.BlockSpec(memory_space=pl.ANY)] * len(values),
        out_specs=[pl.BlockSpec(memory_space=pl.ANY)] * len(values),
        input_output_aliases={i: i for i in range(len(values))},
        cost_estimate=pl.CostEstimate(flops=0, bytes_accessed=0, transcendentals=0),
        compiler_params=pltpu.CompilerParams(vmem_limit_bytes=2**20),
    )(*values)


def expert_kernel(sides, blocks, *refs):
    inputs, refs = refs[:sides], refs[sides:]
    grads, refs = refs[:sides], refs[sides:]
    named, up_a, up_b, down_a, down_b, clock, *refs = refs
    outs, (clock_out, held, scaled, total) = refs[:sides], refs[sides:]
    step = pl.program_id(0)
    rows = inputs[0].shape[0]

    @pl.when(step == 0)
    def _():
        for side in range(sides):
            held[pl.ds(side * rows, rows), :] = inputs[side][...]

    @pl.when(step % blocks == 0)
    def _():
        expert = named[step // blocks]
        width = held.shape[1]
        padded = grads[0].shape[1] - width
        lane = lax.broadcasted_iota(jnp.int32, (rows, padded), 1)
        unit = jnp.where(
            lane == expert, 1 / 256, jnp.where(lane == expert + padded // 2, 1 / 65536, 0.0)
        )
        for side in range(sides):
            halves = grads[side][:, width:].astype(jnp.float32)
            share = jnp.sum(halves * unit, axis=1, keepdims=True)
            scaled[pl.ds(side * rows, rows), :] = (
                share * grads[side][:, :width].astype(jnp.float32)
            ).astype(jnp.bfloat16)

    def block(w_up, w_down):
        pre = lax.dot_general(held[...], w_up[...], NT, preferred_element_type=jnp.float32)
        hidden = lax.dot_general(
            scaled[...], w_down[...], NT, preferred_element_type=jnp.float32
        )
        pre_grad = (hidden * 2.0 * jnp.maximum(pre, 0.0)).astype(jnp.bfloat16)
        return jnp.dot(pre_grad, w_up[...], preferred_element_type=jnp.float32)

    @pl.when(step == 0)
    def _():
        total[...] = block(up_a, down_a)

    @pl.when((step > 0) & (step < blocks))
    def _():
        total[...] += block(up_a, down_a)

    @pl.when((step >= blocks) & (step < 2 * blocks - 1))
    def _():
        total[...] += block(up_b, down_b)

    @pl.when(step == 2 * blocks - 1)
    def _():
        out = total[...] + block(up_b, down_b)
        for side in range(sides):
            outs[side][...] = out[side * rows : (side + 1) * rows].astype(jnp.bfloat16)


def experts(inputs, grads, named, w_up, w_down, clock):
    sides = len(inputs)
    rows, width = inputs[0].shape
    hidden_units = w_down[0].shape[0]
    blocks = BLOCKS
    block = hidden_units // blocks
    whole = pl.BlockSpec((rows, width), lambda step: (0, 0))
    anywhere = pl.BlockSpec(memory_space=pl.ANY)
    first = lambda step: jnp.minimum(step, blocks - 1)
    second = lambda step: jnp.maximum(step - blocks, 0)
    *outs, clock = pl.pallas_call(
        functools.partial(expert_kernel, sides, blocks),
        grid=(CORES * blocks,),
        out_shape=[jax.ShapeDtypeStruct((rows, width), jnp.bfloat16)] * sides
        + [jax.ShapeDtypeStruct(clock.shape, clock.dtype)],
        in_specs=[whole] * sides
        + [pl.BlockSpec(grads[0].shape, lambda step: (0, 0))] * sides
        + [
            pl.BlockSpec(memory_space=pltpu.SMEM),
            pl.BlockSpec((block, width), lambda step: (first(step), 0)),
            pl.BlockSpec((block, width), lambda step: (second(step), 0)),
            pl.BlockSpec((block, width), lambda step: (first(step), 0)),
            pl.BlockSpec((block, width), lambda step: (second(step), 0)),
            anywhere,
        ],
        out_specs=[whole] * sides + [anywhere],
        scratch_shapes=[
            pltpu.VMEM((sides * rows, width), jnp.bfloat16),
            pltpu.VMEM((sides * rows, width), jnp.bfloat16),
            pltpu.VMEM((sides * rows, width), jnp.float32),
        ],
        input_output_aliases={2 * sides + 5: sides},
        compiler_params=pltpu.CompilerParams(vmem_limit_bytes=VMEM_BYTES),
        cost_estimate=pl.CostEstimate(
            flops=12 * sides * rows * width * hidden_units,
            bytes_accessed=8 * width * hidden_units,
            transcendentals=0,
        ),
    )(*inputs, *grads, named, *w_up, *w_down, clock)
    return outs, clock


def dequant_kernel(values, scales, clock, out):
    count, columns = values.shape
    wide = values[...].astype(jnp.float32).reshape(count // SB, SB, columns)
    out[...] = (wide * scales[...][:, None, :]).reshape(count, columns).astype(jnp.bfloat16)


def dequant(values, scales, clock):
    count, columns = values.shape
    steps = 7
    wide = columns // steps
    scales = jnp.repeat(scales, SB, axis=1)
    return pl.pallas_call(
        dequant_kernel,
        grid=(steps,),
        out_shape=jax.ShapeDtypeStruct((count, columns), jnp.bfloat16),
        in_specs=[
            pl.BlockSpec((count, wide), lambda i: (0, i)),
            pl.BlockSpec((count // SB, wide), lambda i: (0, i)),
            pl.BlockSpec(memory_space=pl.ANY),
        ],
        out_specs=pl.BlockSpec((count, wide), lambda i: (0, i)),
        cost_estimate=pl.CostEstimate(
            flops=3804900000, bytes_accessed=0, transcendentals=0
        ),
        compiler_params=pltpu.CompilerParams(vmem_limit_bytes=VMEM_BYTES),
    )(values, scales, clock)


def with_gates(out_grad, expert_ids, gate_fixed, experts, padded):
    hit = expert_ids[:, :, None] == jnp.arange(experts, dtype=jnp.int32)[None, None, :]
    table = jnp.sum(jnp.where(hit, gate_fixed[:, :, None], 0), axis=1)
    halves = jnp.stack([table // 256, table % 256], axis=1).astype(jnp.bfloat16)
    halves = jnp.pad(halves, ((0, 0), (0, 0), (0, padded // 2 - experts)))
    return jnp.concatenate([out_grad, halves.reshape(-1, padded)], axis=1)


def shards(
    saved_inputs, out_grad, expert_ids, gate_fixed, up_values, up_scales, down_values, down_scales
):
    groups, sides = lax.axis_size("group"), lax.axis_size("x")
    tok_dev, width = saved_inputs.shape
    last = groups - 1
    others = range(1, sides)
    both = range(2)
    along, across = {}, {}
    clock = [jnp.zeros((8, 128), jnp.float32)]
    count = groups * sides * CORES
    padded = -(-2 * count // LANES) * LANES
    pair = (lax.axis_index("group") * sides + lax.axis_index("x")) * CORES
    core = lax.axis_index("core")
    named = jnp.stack([pair + core, pair + (core + 1) % CORES]).astype(jnp.int32)
    sources = (saved_inputs, with_gates(out_grad, expert_ids, gate_fixed, count, padded))

    def tick(*values):
        *values, clock[0] = in_order((*values, clock[0]))
        return values

    def spread(kind, step):
        value = along[kind, step]
        if step < last:
            with jax.named_scope(f"gather_z{step + 1}"):
                along[kind, step + 1] = shift(value, "group", 1)
        if not (kind == 1 and step == last):
            for side in others:
                with jax.named_scope(f"gather_x{step}"):
                    across[kind, step, side] = shift(value, "x", side)

    def arrive(kind, step, *more):
        keys = [(along, (kind, step + 1))] if step < last else []
        keys += [(across, (kind, step, side)) for side in others]
        values = tick(*(store[key] for store, key in keys), *more)
        for (store, key), value in zip(keys, values):
            store[key] = value
        if step < last:
            spread(kind, step + 1)
        if kind == 1 and step == last - 1:
            for side in others:
                with jax.named_scope(f"gather_z{step + 1}"):
                    across[kind, last, side] = shift(across[kind, step, side], "group", 1)
        return values[len(keys) :]

    rows, sent, totals = {}, {}, {}

    for kind, source in enumerate(sources):
        along[kind, 0] = source
        spread(kind, 0)
    w_up, w_down = [], []

    def compute(step):
        inputs, grads = (
            [along[kind, step]] + [across[kind, step, side] for side in others] for kind in both
        )
        rows[step], clock[0] = experts(inputs, grads, named, w_up, w_down, clock[0])

    def send_across(step):
        with jax.named_scope(f"reduce_x{step}"):
            sent[step] = [shift(rows[step][side], "x", -side) for side in others]

    def gather_sum(step):
        part = rows[step][0].astype(jnp.float32)
        for value in tick(*sent[step]):
            part = part + value.astype(jnp.float32)
        return part

    def forward(step, total):
        with jax.named_scope(f"reduce_z{step}"):
            return shift(total.astype(jnp.bfloat16), "group", 1)

    def pass_on(step):
        part = gather_sum(step)
        if step > 1:
            part = part + tick(totals[step - 1])[0].astype(jnp.float32)
        totals[step] = forward(step, part)

    raw_up, raw_down = up_values[0].T, down_values[0]
    scales = jnp.stack([up_scales[0].T, down_scales[0]])
    (other_scales,) = tick(shift(scales, "core", 1))
    other_up = shift(raw_up, "core", 1)
    (other_up,) = arrive(0, 0, other_up)
    other_down = shift(raw_down, "core", 1)
    w_up.append(dequant(raw_up, scales[0], clock[0]))
    w_down.append(dequant(raw_down, scales[1], clock[0]))
    other_down, w_up[0], w_down[0] = arrive(1, 0, other_down, w_up[0], w_down[0])
    w_up.append(dequant(other_up, other_scales[0], clock[0]))
    for step in range(1, groups):
        if step == 1:
            (w_up[1],) = arrive(0, step, w_up[1])
            w_down += tick(dequant(other_down, other_scales[1], clock[0]))
        else:
            arrive(0, step)
        if step >= 2:
            send_across(step - 1)
        if step == 2:
            compute(0)
        if step > 2:
            pass_on(step - 2)
        arrive(1, step)
        compute(step)
    pass_on(last - 1)
    send_across(last)
    send_across(0)
    pass_on(last)
    total = tick(totals[last])[0]
    return (total.astype(jnp.float32) + gather_sum(0)).astype(jnp.bfloat16)


def solution(mesh):
    dp, groups, experts = mesh.devices.shape
    fine = Mesh(
        mesh.devices.reshape(dp, groups, experts // CORES, CORES), ("dp", "group", "x", "core")
    )
    tokens = P(("dp", "group", "x", "core"), None)
    weights = P(("group", "x", "core"), None, None)
    return jax.shard_map(
        shards,
        mesh=fine,
        in_specs=(tokens,) * 4 + (weights,) * 4,
        out_specs=tokens,
        check_vma=False,
    )
```

```python
import functools

import jax
import jax.numpy as jnp
from jax import lax
from jax.experimental import pallas as pl
from jax.experimental.pallas import tpu as pltpu
from jax.sharding import Mesh, PartitionSpec as P

SB = 32
CORES = 2
LANES = 128
BLOCKS = 2
PART = 64
VMEM_BYTES = 40 * 2**20
NT = (((1,), (1,)), ((), ()))


def shift(value, axis, by):
    size = lax.axis_size(axis)
    return lax.ppermute(value, axis, [(i, (i + by) % size) for i in range(size)])


def nothing(*refs):
    pass


def in_order(values):
    return pl.pallas_call(
        nothing,
        out_shape=[jax.ShapeDtypeStruct(value.shape, value.dtype) for value in values],
        in_specs=[pl.BlockSpec(memory_space=pl.ANY)] * len(values),
        out_specs=[pl.BlockSpec(memory_space=pl.ANY)] * len(values),
        input_output_aliases={i: i for i in range(len(values))},
        cost_estimate=pl.CostEstimate(flops=0, bytes_accessed=0, transcendentals=0),
        compiler_params=pltpu.CompilerParams(vmem_limit_bytes=2**20),
    )(*values)


def expert_kernel(pieces, sides, blocks, *refs):
    inputs, refs = refs[:pieces], refs[pieces:]
    grads, refs = refs[:sides], refs[sides:]
    named, up_a, up_b, down_a, down_b, clock, *refs = refs
    outs, (clock_out, held, scaled, total) = refs[:sides], refs[sides:]
    step = pl.program_id(0)
    rows = outs[0].shape[0]

    @pl.when(step == 0)
    def _():
        first = 0
        for piece in inputs:
            held[pl.ds(first, piece.shape[0]), :] = piece[...]
            first += piece.shape[0]

    @pl.when(step % blocks == 0)
    def _():
        expert = named[step // blocks]
        width = held.shape[1]
        padded = grads[0].shape[1] - width
        lane = lax.broadcasted_iota(jnp.int32, (rows, padded), 1)
        unit = jnp.where(
            lane == expert, 1 / 256, jnp.where(lane == expert + padded // 2, 1 / 65536, 0.0)
        )
        for side in range(sides):
            halves = grads[side][:, width:].astype(jnp.float32)
            share = jnp.sum(halves * unit, axis=1, keepdims=True)
            scaled[pl.ds(side * rows, rows), :] = (
                share * grads[side][:, :width].astype(jnp.float32)
            ).astype(jnp.bfloat16)

    def block(w_up, w_down):
        pre = lax.dot_general(held[...], w_up[...], NT, preferred_element_type=jnp.float32)
        hidden = lax.dot_general(
            scaled[...], w_down[...], NT, preferred_element_type=jnp.float32
        )
        pre_grad = (hidden * 2.0 * jnp.maximum(pre, 0.0)).astype(jnp.bfloat16)
        return jnp.dot(pre_grad, w_up[...], preferred_element_type=jnp.float32)

    @pl.when(step == 0)
    def _():
        total[...] = block(up_a, down_a)

    @pl.when((step > 0) & (step < blocks))
    def _():
        total[...] += block(up_a, down_a)

    @pl.when((step >= blocks) & (step < 2 * blocks - 1))
    def _():
        total[...] += block(up_b, down_b)

    @pl.when(step == 2 * blocks - 1)
    def _():
        out = total[...] + block(up_b, down_b)
        for side in range(sides):
            outs[side][...] = out[side * rows : (side + 1) * rows].astype(jnp.bfloat16)


def experts(inputs, grads, named, w_up, w_down, clock):
    pieces, sides = len(inputs), len(grads)
    rows, width = grads[0].shape[0], w_down[0].shape[1]
    hidden_units = w_down[0].shape[0]
    blocks = BLOCKS
    block = hidden_units // blocks
    whole = pl.BlockSpec((rows, width), lambda step: (0, 0))
    anywhere = pl.BlockSpec(memory_space=pl.ANY)
    first = lambda step: jnp.minimum(step, blocks - 1)
    second = lambda step: jnp.maximum(step - blocks, 0)
    *outs, clock = pl.pallas_call(
        functools.partial(expert_kernel, pieces, sides, blocks),
        grid=(CORES * blocks,),
        out_shape=[jax.ShapeDtypeStruct((rows, width), jnp.bfloat16)] * sides
        + [jax.ShapeDtypeStruct(clock.shape, clock.dtype)],
        in_specs=[pl.BlockSpec(piece.shape, lambda step: (0, 0)) for piece in (*inputs, *grads)]
        + [
            pl.BlockSpec(memory_space=pltpu.SMEM),
            pl.BlockSpec((block, width), lambda step: (first(step), 0)),
            pl.BlockSpec((block, width), lambda step: (second(step), 0)),
            pl.BlockSpec((block, width), lambda step: (first(step), 0)),
            pl.BlockSpec((block, width), lambda step: (second(step), 0)),
            anywhere,
        ],
        out_specs=[whole] * sides + [anywhere],
        scratch_shapes=[
            pltpu.VMEM((sides * rows, width), jnp.bfloat16),
            pltpu.VMEM((sides * rows, width), jnp.bfloat16),
            pltpu.VMEM((sides * rows, width), jnp.float32),
        ],
        input_output_aliases={pieces + sides + 5: sides},
        compiler_params=pltpu.CompilerParams(vmem_limit_bytes=VMEM_BYTES),
        cost_estimate=pl.CostEstimate(
            flops=12 * sides * rows * width * hidden_units,
            bytes_accessed=8 * width * hidden_units,
            transcendentals=0,
        ),
    )(*inputs, *grads, named, *w_up, *w_down, clock)
    return outs, clock


def dequant_kernel(values, scales, clock, out):
    count, columns = values.shape
    wide = values[...].astype(jnp.float32).reshape(count // SB, SB, columns)
    out[...] = (wide * scales[...][:, None, :]).reshape(count, columns).astype(jnp.bfloat16)


def dequant(values, scales, clock):
    count, columns = values.shape
    steps = 7
    wide = columns // steps
    scales = jnp.repeat(scales, SB, axis=1)
    return pl.pallas_call(
        dequant_kernel,
        grid=(steps,),
        out_shape=jax.ShapeDtypeStruct((count, columns), jnp.bfloat16),
        in_specs=[
            pl.BlockSpec((count, wide), lambda i: (0, i)),
            pl.BlockSpec((count // SB, wide), lambda i: (0, i)),
            pl.BlockSpec(memory_space=pl.ANY),
        ],
        out_specs=pl.BlockSpec((count, wide), lambda i: (0, i)),
        cost_estimate=pl.CostEstimate(
            flops=3804900000, bytes_accessed=0, transcendentals=0
        ),
        compiler_params=pltpu.CompilerParams(vmem_limit_bytes=VMEM_BYTES),
    )(values, scales, clock)


def with_gates(out_grad, expert_ids, gate_fixed, experts, padded):
    hit = expert_ids[:, :, None] == jnp.arange(experts, dtype=jnp.int32)[None, None, :]
    table = jnp.sum(jnp.where(hit, gate_fixed[:, :, None], 0), axis=1)
    halves = jnp.stack([table // 256, table % 256], axis=1).astype(jnp.bfloat16)
    halves = jnp.pad(halves, ((0, 0), (0, 0), (0, padded // 2 - experts)))
    return jnp.concatenate([out_grad, halves.reshape(-1, padded)], axis=1)


def shards(
    saved_inputs, out_grad, expert_ids, gate_fixed, up_values, up_scales, down_values, down_scales
):
    groups, sides = lax.axis_size("group"), lax.axis_size("x")
    tok_dev, width = saved_inputs.shape
    last = groups - 1
    others = range(1, sides)
    both = range(2)
    along, across = {}, {}
    clock = [jnp.zeros((8, 128), jnp.float32)]
    count = groups * sides * CORES
    padded = -(-2 * count // LANES) * LANES
    pair = (lax.axis_index("group") * sides + lax.axis_index("x")) * CORES
    core = lax.axis_index("core")
    named = jnp.stack([pair + core, pair + (core + 1) % CORES]).astype(jnp.int32)
    sources = (saved_inputs, with_gates(out_grad, expert_ids, gate_fixed, count, padded))

    def tick(*values):
        *values, clock[0] = in_order((*values, clock[0]))
        return values

    def spread(kind, step):
        value = along[kind, step]
        if step < last:
            with jax.named_scope(f"gather_z{step + 1}"):
                along[kind, step + 1] = shift(value, "group", 1)
        if not (kind == 1 and step == last):
            rest = value if step < last else value[PART:]
            for side in others:
                with jax.named_scope(f"gather_x{step}"):
                    across[kind, step, side, 1] = shift(rest, "x", side)

    def arrive(kind, step, *more):
        keys = [(along, (kind, step + 1))] if step < last else []
        keys += [(across, key) for key in sorted(across) if key[:2] == (kind, step)]
        values = tick(*(store[key] for store, key in keys), *more)
        for (store, key), value in zip(keys, values):
            store[key] = value
        if step < last:
            spread(kind, step + 1)
        if step == last - 1:
            for side in others:
                value = across[kind, step, side, 1]
                value = value if kind == 1 else value[:PART]
                with jax.named_scope(f"gather_z{step + 1}"):
                    across[kind, last, side, 0] = shift(value, "group", 1)
        return values[len(keys) :]

    rows, sent, totals = {}, {}, {}

    for kind, source in enumerate(sources):
        along[kind, 0] = source
        spread(kind, 0)
    w_up, w_down = [], []

    def compute(step):
        inputs, grads = (
            [along[kind, step]]
            + [across[key] for key in sorted(across) if key[:2] == (kind, step)]
            for kind in both
        )
        rows[step], clock[0] = experts(inputs, grads, named, w_up, w_down, clock[0])

    def send_across(step):
        with jax.named_scope(f"reduce_x{step}"):
            sent[step] = [shift(rows[step][side], "x", -side) for side in others]

    def gather_sum(step):
        part = rows[step][0].astype(jnp.float32)
        for value in tick(*sent[step]):
            part = part + value.astype(jnp.float32)
        return part

    def forward(step, total):
        with jax.named_scope(f"reduce_z{step}"):
            return shift(total.astype(jnp.bfloat16), "group", 1)

    def pass_on(step):
        part = gather_sum(step)
        if step > 1:
            part = part + tick(totals[step - 1])[0].astype(jnp.float32)
        totals[step] = forward(step, part)

    raw_up, raw_down = up_values[0].T, down_values[0]
    scales = jnp.stack([up_scales[0].T, down_scales[0]])
    other_scales, other_up = tick(shift(scales, "core", 1), shift(raw_up, "core", 1))
    arrive(0, 0)
    other_down = shift(raw_down, "core", 1)
    w_up.append(dequant(raw_up, scales[0], clock[0]))
    w_down.append(dequant(raw_down, scales[1], clock[0]))
    w_up[0], w_down[0] = arrive(1, 0, w_up[0], w_down[0])
    w_up.append(dequant(other_up, other_scales[0], clock[0]))
    for step in range(1, groups):
        if step > 2:
            pass_on(step - 2)
        if step == 1:
            w_up[1], other_down = arrive(0, step, w_up[1], other_down)
            w_down += tick(dequant(other_down, other_scales[1], clock[0]))
        else:
            arrive(0, step)
        if step >= 2:
            send_across(step - 1)
        if step == 2:
            compute(0)
        arrive(1, step)
        compute(step)
    pass_on(last - 1)
    send_across(last)
    send_across(0)
    pass_on(last)
    total = tick(totals[last])[0]
    return (total.astype(jnp.float32) + gather_sum(0)).astype(jnp.bfloat16)


def solution(mesh):
    dp, groups, experts = mesh.devices.shape
    fine = Mesh(
        mesh.devices.reshape(dp, groups, experts // CORES, CORES), ("dp", "group", "x", "core")
    )
    tokens = P(("dp", "group", "x", "core"), None)
    weights = P(("group", "x", "core"), None, None)
    return jax.shard_map(
        shards,
        mesh=fine,
        in_specs=(tokens,) * 4 + (weights,) * 4,
        out_specs=tokens,
        check_vma=False,
    )
```

```python
import functools

import jax
import jax.numpy as jnp
from jax import lax
from jax.experimental import pallas as pl
from jax.experimental.pallas import tpu as pltpu
from jax.sharding import Mesh, PartitionSpec as P

SB = 32
CORES = 2
LANES = 128
BLOCKS = 2
PART = 64
WAIT_COST = 76 * 10**8
VMEM_BYTES = 40 * 2**20
NT = (((1,), (1,)), ((), ()))


def shift(value, axis, by):
    size = lax.axis_size(axis)
    return lax.ppermute(value, axis, [(i, (i + by) % size) for i in range(size)])


def nothing(*refs):
    pass


def in_order(values, cost=0):
    return pl.pallas_call(
        nothing,
        out_shape=[jax.ShapeDtypeStruct(value.shape, value.dtype) for value in values],
        in_specs=[pl.BlockSpec(memory_space=pl.ANY)] * len(values),
        out_specs=[pl.BlockSpec(memory_space=pl.ANY)] * len(values),
        input_output_aliases={i: i for i in range(len(values))},
        cost_estimate=pl.CostEstimate(flops=cost, bytes_accessed=0, transcendentals=0),
        compiler_params=pltpu.CompilerParams(vmem_limit_bytes=2**20),
    )(*values)


def expert_kernel(pieces, sides, blocks, *refs):
    inputs, refs = refs[:pieces], refs[pieces:]
    grads, refs = refs[:sides], refs[sides:]
    named, up_a, up_b, down_a, down_b, clock, *refs = refs
    outs, (clock_out, held, scaled, total) = refs[:sides], refs[sides:]
    step = pl.program_id(0)
    rows = outs[0].shape[0]

    @pl.when(step == 0)
    def _():
        first = 0
        for piece in inputs:
            held[pl.ds(first, piece.shape[0]), :] = piece[...]
            first += piece.shape[0]

    @pl.when(step % blocks == 0)
    def _():
        expert = named[step // blocks]
        width = held.shape[1]
        padded = grads[0].shape[1] - width
        lane = lax.broadcasted_iota(jnp.int32, (rows, padded), 1)
        unit = jnp.where(
            lane == expert, 1 / 256, jnp.where(lane == expert + padded // 2, 1 / 65536, 0.0)
        )
        for side in range(sides):
            halves = grads[side][:, width:].astype(jnp.float32)
            share = jnp.sum(halves * unit, axis=1, keepdims=True)
            scaled[pl.ds(side * rows, rows), :] = (
                share * grads[side][:, :width].astype(jnp.float32)
            ).astype(jnp.bfloat16)

    def block(w_up, w_down):
        pre = lax.dot_general(held[...], w_up[...], NT, preferred_element_type=jnp.float32)
        hidden = lax.dot_general(
            scaled[...], w_down[...], NT, preferred_element_type=jnp.float32
        )
        pre_grad = (hidden * 2.0 * jnp.maximum(pre, 0.0)).astype(jnp.bfloat16)
        return jnp.dot(pre_grad, w_up[...], preferred_element_type=jnp.float32)

    @pl.when(step == 0)
    def _():
        total[...] = block(up_a, down_a)

    @pl.when((step > 0) & (step < blocks))
    def _():
        total[...] += block(up_a, down_a)

    @pl.when((step >= blocks) & (step < 2 * blocks - 1))
    def _():
        total[...] += block(up_b, down_b)

    @pl.when(step == 2 * blocks - 1)
    def _():
        out = total[...] + block(up_b, down_b)
        for side in range(sides):
            outs[side][...] = out[side * rows : (side + 1) * rows].astype(jnp.bfloat16)


def experts(inputs, grads, named, w_up, w_down, clock):
    pieces, sides = len(inputs), len(grads)
    rows, width = grads[0].shape[0], w_down[0].shape[1]
    hidden_units = w_down[0].shape[0]
    blocks = BLOCKS
    block = hidden_units // blocks
    whole = pl.BlockSpec((rows, width), lambda step: (0, 0))
    anywhere = pl.BlockSpec(memory_space=pl.ANY)
    first = lambda step: jnp.minimum(step, blocks - 1)
    second = lambda step: jnp.maximum(step - blocks, 0)
    *outs, clock = pl.pallas_call(
        functools.partial(expert_kernel, pieces, sides, blocks),
        grid=(CORES * blocks,),
        out_shape=[jax.ShapeDtypeStruct((rows, width), jnp.bfloat16)] * sides
        + [jax.ShapeDtypeStruct(clock.shape, clock.dtype)],
        in_specs=[pl.BlockSpec(piece.shape, lambda step: (0, 0)) for piece in (*inputs, *grads)]
        + [
            pl.BlockSpec(memory_space=pltpu.SMEM),
            pl.BlockSpec((block, width), lambda step: (first(step), 0)),
            pl.BlockSpec((block, width), lambda step: (second(step), 0)),
            pl.BlockSpec((block, width), lambda step: (first(step), 0)),
            pl.BlockSpec((block, width), lambda step: (second(step), 0)),
            anywhere,
        ],
        out_specs=[whole] * sides + [anywhere],
        scratch_shapes=[
            pltpu.VMEM((sides * rows, width), jnp.bfloat16),
            pltpu.VMEM((sides * rows, width), jnp.bfloat16),
            pltpu.VMEM((sides * rows, width), jnp.float32),
        ],
        input_output_aliases={pieces + sides + 5: sides},
        compiler_params=pltpu.CompilerParams(vmem_limit_bytes=VMEM_BYTES),
        cost_estimate=pl.CostEstimate(
            flops=12 * sides * rows * width * hidden_units,
            bytes_accessed=8 * width * hidden_units,
            transcendentals=0,
        ),
    )(*inputs, *grads, named, *w_up, *w_down, clock)
    return outs, clock


def dequant_kernel(values, scales, clock, out):
    count, columns = values.shape
    wide = values[...].astype(jnp.float32).reshape(count // SB, SB, columns)
    out[...] = (wide * scales[...][:, None, :]).reshape(count, columns).astype(jnp.bfloat16)


def dequant(values, scales, clock):
    count, columns = values.shape
    steps = 7
    wide = columns // steps
    scales = jnp.repeat(scales, SB, axis=1)
    return pl.pallas_call(
        dequant_kernel,
        grid=(steps,),
        out_shape=jax.ShapeDtypeStruct((count, columns), jnp.bfloat16),
        in_specs=[
            pl.BlockSpec((count, wide), lambda i: (0, i)),
            pl.BlockSpec((count // SB, wide), lambda i: (0, i)),
            pl.BlockSpec(memory_space=pl.ANY),
        ],
        out_specs=pl.BlockSpec((count, wide), lambda i: (0, i)),
        cost_estimate=pl.CostEstimate(
            flops=3804900000, bytes_accessed=0, transcendentals=0
        ),
        compiler_params=pltpu.CompilerParams(vmem_limit_bytes=VMEM_BYTES),
    )(values, scales, clock)


def with_gates(out_grad, expert_ids, gate_fixed, experts, padded):
    hit = expert_ids[:, :, None] == jnp.arange(experts, dtype=jnp.int32)[None, None, :]
    table = jnp.sum(jnp.where(hit, gate_fixed[:, :, None], 0), axis=1)
    halves = jnp.stack([table // 256, table % 256], axis=1).astype(jnp.bfloat16)
    halves = jnp.pad(halves, ((0, 0), (0, 0), (0, padded // 2 - experts)))
    return jnp.concatenate([out_grad, halves.reshape(-1, padded)], axis=1)


def shards(
    saved_inputs, out_grad, expert_ids, gate_fixed, up_values, up_scales, down_values, down_scales
):
    groups, sides = lax.axis_size("group"), lax.axis_size("x")
    tok_dev, width = saved_inputs.shape
    last = groups - 1
    others = range(1, sides)
    both = range(2)
    along, across = {}, {}
    clock = [jnp.zeros((8, 128), jnp.float32)]
    count = groups * sides * CORES
    padded = -(-2 * count // LANES) * LANES
    pair = (lax.axis_index("group") * sides + lax.axis_index("x")) * CORES
    core = lax.axis_index("core")
    named = jnp.stack([pair + core, pair + (core + 1) % CORES]).astype(jnp.int32)
    sources = (saved_inputs, with_gates(out_grad, expert_ids, gate_fixed, count, padded))

    def tick(*values, cost=0):
        *values, clock[0] = in_order((*values, clock[0]), cost)
        return values

    def spread(kind, step):
        value = along[kind, step]
        if step < last:
            with jax.named_scope(f"gather_z{step + 1}"):
                along[kind, step + 1] = shift(value, "group", 1)
        if not (kind == 1 and step == last):
            rest = value if step < last else value[PART:]
            for side in others:
                with jax.named_scope(f"gather_x{step}"):
                    across[kind, step, side, 1] = shift(rest, "x", side)

    def arrive(kind, step, *more):
        keys = [(along, (kind, step + 1))] if step < last else []
        keys += [(across, key) for key in sorted(across) if key[:2] == (kind, step)]
        values = tick(*(store[key] for store, key in keys), *more)
        for (store, key), value in zip(keys, values):
            store[key] = value
        if step < last:
            spread(kind, step + 1)
        if step == last - 1:
            for side in others:
                value = across[kind, step, side, 1]
                value = value if kind == 1 else value[:PART]
                with jax.named_scope(f"gather_z{step + 1}"):
                    across[kind, last, side, 0] = shift(value, "group", 1)
        return values[len(keys) :]

    rows, sent, totals = {}, {}, {}

    for kind, source in enumerate(sources):
        along[kind, 0] = source
        spread(kind, 0)
    w_up, w_down = [], []

    def compute(step):
        inputs, grads = (
            [along[kind, step]]
            + [across[key] for key in sorted(across) if key[:2] == (kind, step)]
            for kind in both
        )
        rows[step], clock[0] = experts(inputs, grads, named, w_up, w_down, clock[0])

    def send_across(step):
        with jax.named_scope(f"reduce_x{step}"):
            sent[step] = [shift(rows[step][side], "x", -side) for side in others]

    def gather_sum(step):
        part = rows[step][0].astype(jnp.float32)
        for value in tick(*sent[step]):
            part = part + value.astype(jnp.float32)
        return part

    def forward(step, total):
        with jax.named_scope(f"reduce_z{step}"):
            return shift(total.astype(jnp.bfloat16), "group", 1)

    def pass_on(step):
        part = gather_sum(step)
        if step > 1:
            part = part + tick(totals[step - 1])[0].astype(jnp.float32)
        totals[step] = forward(step, part)

    raw_up, raw_down = up_values[0].T, down_values[0]
    scales = jnp.stack([up_scales[0].T, down_scales[0]])
    other_scales, other_up = tick(shift(scales, "core", 1), shift(raw_up, "core", 1))
    arrive(0, 0)
    other_down = shift(raw_down, "core", 1)
    w_up.append(dequant(raw_up, scales[0], clock[0]))
    w_down.append(dequant(raw_down, scales[1], clock[0]))
    w_up[0], w_down[0] = arrive(1, 0, w_up[0], w_down[0])
    w_up.append(dequant(other_up, other_scales[0], clock[0]))
    for step in range(1, groups):
        if step > 2:
            pass_on(step - 2)
        if step == 1:
            w_up[1], other_down = arrive(0, step, w_up[1], other_down)
            w_down += tick(dequant(other_down, other_scales[1], clock[0]))
        else:
            arrive(0, step)
        if step >= 2:
            send_across(step - 1)
        if step == 2:
            compute(0)
        arrive(1, step)
        compute(step)
    halves = [slice(0, tok_dev // 2), slice(tok_dev // 2, tok_dev)]
    with jax.named_scope(f"reduce_x{last}"):
        sent[last] = [
            [shift(rows[last][side][half], "x", -side) for side in others] for half in halves
        ]
    pass_on(last - 1)
    (total, *own) = tick(totals[last - 1], *rows[0][1:])
    rows[0] = [rows[0][0], *own]
    passed = []
    for half, values in zip(halves, sent[last]):
        part = rows[last][0][half].astype(jnp.float32) + total[half].astype(jnp.float32)
        for value in tick(*values):
            part = part + value.astype(jnp.float32)
        passed.append(forward(last, part))
    send_across(0)
    passed = [tick(value, cost=WAIT_COST)[0] for value in passed]
    own = gather_sum(0)
    passed = [value.astype(jnp.float32) + own[half] for half, value in zip(halves, passed)]
    return jnp.concatenate(passed, axis=0).astype(jnp.bfloat16)


def solution(mesh):
    dp, groups, experts = mesh.devices.shape
    fine = Mesh(
        mesh.devices.reshape(dp, groups, experts // CORES, CORES), ("dp", "group", "x", "core")
    )
    tokens = P(("dp", "group", "x", "core"), None)
    weights = P(("group", "x", "core"), None, None)
    return jax.shard_map(
        shards,
        mesh=fine,
        in_specs=(tokens,) * 4 + (weights,) * 4,
        out_specs=tokens,
        check_vma=False,
    )
```

```python
import functools

import jax
import jax.numpy as jnp
from jax import lax
from jax.experimental import pallas as pl
from jax.experimental.pallas import tpu as pltpu
from jax.sharding import Mesh, PartitionSpec as P

SB = 32
CORES = 2
LANES = 128
BLOCKS = 2
PART = 64
WAIT_COST = 76 * 10**8
VMEM_BYTES = 40 * 2**20
NT = (((1,), (1,)), ((), ()))


def shift(value, axis, by):
    size = lax.axis_size(axis)
    return lax.ppermute(value, axis, [(i, (i + by) % size) for i in range(size)])


def nothing(*refs):
    pass


def in_order(values, cost=0):
    return pl.pallas_call(
        nothing,
        out_shape=[jax.ShapeDtypeStruct(value.shape, value.dtype) for value in values],
        in_specs=[pl.BlockSpec(memory_space=pl.ANY)] * len(values),
        out_specs=[pl.BlockSpec(memory_space=pl.ANY)] * len(values),
        input_output_aliases={i: i for i in range(len(values))},
        cost_estimate=pl.CostEstimate(flops=cost, bytes_accessed=0, transcendentals=0),
        compiler_params=pltpu.CompilerParams(vmem_limit_bytes=2**20),
    )(*values)


def expert_kernel(pieces, sides, blocks, *refs):
    inputs, refs = refs[:pieces], refs[pieces:]
    grads, refs = refs[:sides], refs[sides:]
    named, up_a, up_b, down_a, down_b, clock, *refs = refs
    outs, (clock_out, held, scaled, total) = refs[:sides], refs[sides:]
    step = pl.program_id(0)
    rows = outs[0].shape[0]

    @pl.when(step == 0)
    def _():
        first = 0
        for piece in inputs:
            held[pl.ds(first, piece.shape[0]), :] = piece[...]
            first += piece.shape[0]

    @pl.when(step % blocks == 0)
    def _():
        expert = named[step // blocks]
        width = held.shape[1]
        padded = grads[0].shape[1] - width
        lane = lax.broadcasted_iota(jnp.int32, (rows, padded), 1)
        unit = jnp.where(
            lane == expert, 1 / 256, jnp.where(lane == expert + padded // 2, 1 / 65536, 0.0)
        )
        for side in range(sides):
            halves = grads[side][:, width:].astype(jnp.float32)
            share = jnp.sum(halves * unit, axis=1, keepdims=True)
            scaled[pl.ds(side * rows, rows), :] = (
                share * grads[side][:, :width].astype(jnp.float32)
            ).astype(jnp.bfloat16)

    def block(w_up, w_down):
        pre = lax.dot_general(held[...], w_up[...], NT, preferred_element_type=jnp.float32)
        hidden = lax.dot_general(
            scaled[...], w_down[...], NT, preferred_element_type=jnp.float32
        )
        pre_grad = (hidden * 2.0 * jnp.maximum(pre, 0.0)).astype(jnp.bfloat16)
        return jnp.dot(pre_grad, w_up[...], preferred_element_type=jnp.float32)

    @pl.when(step == 0)
    def _():
        total[...] = block(up_a, down_a)

    @pl.when((step > 0) & (step < blocks))
    def _():
        total[...] += block(up_a, down_a)

    @pl.when((step >= blocks) & (step < 2 * blocks - 1))
    def _():
        total[...] += block(up_b, down_b)

    @pl.when(step == 2 * blocks - 1)
    def _():
        out = total[...] + block(up_b, down_b)
        for side in range(sides):
            outs[side][...] = out[side * rows : (side + 1) * rows].astype(jnp.bfloat16)


def experts(inputs, grads, named, w_up, w_down, clock):
    pieces, sides = len(inputs), len(grads)
    rows, width = grads[0].shape[0], w_down[0].shape[1]
    hidden_units = w_down[0].shape[0]
    blocks = BLOCKS
    block = hidden_units // blocks
    whole = pl.BlockSpec((rows, width), lambda step: (0, 0))
    anywhere = pl.BlockSpec(memory_space=pl.ANY)
    first = lambda step: jnp.minimum(step, blocks - 1)
    second = lambda step: jnp.maximum(step - blocks, 0)
    *outs, clock = pl.pallas_call(
        functools.partial(expert_kernel, pieces, sides, blocks),
        grid=(CORES * blocks,),
        out_shape=[jax.ShapeDtypeStruct((rows, width), jnp.bfloat16)] * sides
        + [jax.ShapeDtypeStruct(clock.shape, clock.dtype)],
        in_specs=[pl.BlockSpec(piece.shape, lambda step: (0, 0)) for piece in (*inputs, *grads)]
        + [
            pl.BlockSpec(memory_space=pltpu.SMEM),
            pl.BlockSpec((block, width), lambda step: (first(step), 0)),
            pl.BlockSpec((block, width), lambda step: (second(step), 0)),
            pl.BlockSpec((block, width), lambda step: (first(step), 0)),
            pl.BlockSpec((block, width), lambda step: (second(step), 0)),
            anywhere,
        ],
        out_specs=[whole] * sides + [anywhere],
        scratch_shapes=[
            pltpu.VMEM((sides * rows, width), jnp.bfloat16),
            pltpu.VMEM((sides * rows, width), jnp.bfloat16),
            pltpu.VMEM((sides * rows, width), jnp.float32),
        ],
        input_output_aliases={pieces + sides + 5: sides},
        compiler_params=pltpu.CompilerParams(vmem_limit_bytes=VMEM_BYTES),
        cost_estimate=pl.CostEstimate(
            flops=12 * sides * rows * width * hidden_units,
            bytes_accessed=8 * width * hidden_units,
            transcendentals=0,
        ),
    )(*inputs, *grads, named, *w_up, *w_down, clock)
    return outs, clock


def dequant_kernel(values, scales, clock, out):
    count, columns = values.shape
    wide = values[...].astype(jnp.float32).reshape(count // SB, SB, columns)
    out[...] = (wide * scales[...][:, None, :]).reshape(count, columns).astype(jnp.bfloat16)


def dequant(values, scales, clock):
    count, columns = values.shape
    steps = 7
    wide = columns // steps
    scales = jnp.repeat(scales, SB, axis=1)
    return pl.pallas_call(
        dequant_kernel,
        grid=(steps,),
        out_shape=jax.ShapeDtypeStruct((count, columns), jnp.bfloat16),
        in_specs=[
            pl.BlockSpec((count, wide), lambda i: (0, i)),
            pl.BlockSpec((count // SB, wide), lambda i: (0, i)),
            pl.BlockSpec(memory_space=pl.ANY),
        ],
        out_specs=pl.BlockSpec((count, wide), lambda i: (0, i)),
        cost_estimate=pl.CostEstimate(
            flops=3804900000, bytes_accessed=0, transcendentals=0
        ),
        compiler_params=pltpu.CompilerParams(vmem_limit_bytes=VMEM_BYTES),
    )(values, scales, clock)


def with_gates(out_grad, expert_ids, gate_fixed, experts, padded):
    hit = expert_ids[:, :, None] == jnp.arange(experts, dtype=jnp.int32)[None, None, :]
    table = jnp.sum(jnp.where(hit, gate_fixed[:, :, None], 0), axis=1)
    halves = jnp.stack([table // 256, table % 256], axis=1).astype(jnp.bfloat16)
    halves = jnp.pad(halves, ((0, 0), (0, 0), (0, padded // 2 - experts)))
    return jnp.concatenate([out_grad, halves.reshape(-1, padded)], axis=1)


def shards(
    saved_inputs, out_grad, expert_ids, gate_fixed, up_values, up_scales, down_values, down_scales
):
    groups, sides = lax.axis_size("group"), lax.axis_size("x")
    tok_dev, width = saved_inputs.shape
    last = groups - 1
    others = range(1, sides)
    both = range(2)
    along, across = {}, {}
    clock = [jnp.zeros((8, 128), jnp.float32)]
    count = groups * sides * CORES
    padded = -(-2 * count // LANES) * LANES
    pair = (lax.axis_index("group") * sides + lax.axis_index("x")) * CORES
    core = lax.axis_index("core")
    named = jnp.stack([pair + core, pair + (core + 1) % CORES]).astype(jnp.int32)
    sources = (saved_inputs, with_gates(out_grad, expert_ids, gate_fixed, count, padded))

    def tick(*values, cost=0):
        *values, clock[0] = in_order((*values, clock[0]), cost)
        return values

    def spread(kind, step):
        value = along[kind, step]
        if step < last:
            with jax.named_scope(f"gather_z{step + 1}"):
                along[kind, step + 1] = shift(value, "group", 1)
        if not (kind == 1 and step == last):
            rest = value if step < last else value[PART:]
            for side in others:
                with jax.named_scope(f"gather_x{step}"):
                    across[kind, step, side, 1] = shift(rest, "x", side)

    def arrive(kind, step, *more):
        keys = [(along, (kind, step + 1))] if step < last else []
        keys += [(across, key) for key in sorted(across) if key[:2] == (kind, step)]
        values = tick(*(store[key] for store, key in keys), *more)
        for (store, key), value in zip(keys, values):
            store[key] = value
        if step < last:
            spread(kind, step + 1)
        if step == last - 1:
            for side in others:
                value = across[kind, step, side, 1]
                value = value if kind == 1 else value[:PART]
                with jax.named_scope(f"gather_z{step + 1}"):
                    across[kind, last, side, 0] = shift(value, "group", 1)
        return values[len(keys) :]

    rows, sent, totals = {}, {}, {}

    for kind, source in enumerate(sources):
        along[kind, 0] = source
        spread(kind, 0)
    w_up, w_down = [], []

    def compute(step):
        inputs, grads = (
            [along[kind, step]]
            + [across[key] for key in sorted(across) if key[:2] == (kind, step)]
            for kind in both
        )
        rows[step], clock[0] = experts(inputs, grads, named, w_up, w_down, clock[0])

    def send_across(step):
        with jax.named_scope(f"reduce_x{step}"):
            sent[step] = [shift(rows[step][side], "x", -side) for side in others]

    def gather_sum(step):
        part = rows[step][0].astype(jnp.float32)
        for value in tick(*sent[step]):
            part = part + value.astype(jnp.float32)
        return part

    def forward(step, total):
        with jax.named_scope(f"reduce_z{step}"):
            return shift(total.astype(jnp.bfloat16), "group", 1)

    def pass_on(step):
        part = gather_sum(step)
        if step > 1:
            part = part + tick(totals[step - 1])[0].astype(jnp.float32)
        totals[step] = forward(step, part)

    raw_up, raw_down = up_values[0].T, down_values[0]
    scales = jnp.stack([up_scales[0].T, down_scales[0]])
    other_scales, other_up = tick(shift(scales, "core", 1), shift(raw_up, "core", 1))
    arrive(0, 0)
    other_down = shift(raw_down, "core", 1)
    w_up.append(dequant(raw_up, scales[0], clock[0]))
    w_down.append(dequant(raw_down, scales[1], clock[0]))
    w_up[0], w_down[0] = arrive(1, 0, w_up[0], w_down[0])
    w_up.append(dequant(other_up, other_scales[0], clock[0]))
    for step in range(1, groups):
        if step > 2:
            pass_on(step - 2)
        if step == 1:
            w_up[1], other_down = arrive(0, step, w_up[1], other_down)
            w_down += tick(dequant(other_down, other_scales[1], clock[0]))
        else:
            arrive(0, step)
        if step >= 2:
            send_across(step - 1)
        if step == 2:
            compute(0)
        arrive(1, step)
        compute(step)
    halves = [slice(0, tok_dev // 2), slice(tok_dev // 2, tok_dev)]
    with jax.named_scope(f"reduce_x{last}"):
        sent[last] = [
            [shift(rows[last][side][half], "x", -side) for side in others] for half in halves
        ]
    pass_on(last - 1)
    (total, *own) = tick(totals[last - 1], *rows[0][1:])
    rows[0] = [rows[0][0], *own]
    passed = []
    for half, values in zip(halves, sent[last]):
        part = rows[last][0][half].astype(jnp.float32) + total[half].astype(jnp.float32)
        for value in tick(*values):
            part = part + value.astype(jnp.float32)
        passed.append(forward(last, part))
    send_across(0)
    passed = [tick(value)[0] for value in passed]
    own = gather_sum(0)
    passed = [value.astype(jnp.float32) + own[half] for half, value in zip(halves, passed)]
    return jnp.concatenate(passed, axis=0).astype(jnp.bfloat16)


def solution(mesh):
    dp, groups, experts = mesh.devices.shape
    fine = Mesh(
        mesh.devices.reshape(dp, groups, experts // CORES, CORES), ("dp", "group", "x", "core")
    )
    tokens = P(("dp", "group", "x", "core"), None)
    weights = P(("group", "x", "core"), None, None)
    return jax.shard_map(
        shards,
        mesh=fine,
        in_specs=(tokens,) * 4 + (weights,) * 4,
        out_specs=tokens,
        check_vma=False,
    )
```
